32 devices in a mesh: orb: 8 (over z, y), grid: 4 (over x, core).
Axes of the slice: x: 2, y: 2, z: 4, core: 2. Of those that a mesh axis runs over, the one named last changes fastest.
Arguments:
- orbitals: float32 [16, 32, 1024], P('orb', 'grid'), may hold values from -6 to 6
- dielectric: float32 [16, 32, 1024], P('orb', 'grid'), may hold values from 1 to 80
- pair_offsets: int32 [16, 4], replicated, may hold values from 0 to 3, each once within a row
- pair_counts: int32 [16], replicated, may hold values from 1 to 4, as said below
- box_shift: int32 [16], replicated, may hold values from 0 to 8
Outputs:
- exchange_action: float32 [16, 32, 1024], P('orb', 'grid')
The draws below stay inside these ranges and needn't reach their ends.
Inputs may be any that keep to these rules, and one draw needn't show every extreme that they name: `pair_counts`: in each aligned block of 8 orbitals the counts sum to 16, and in each such block the 2 orbitals of one owner (an aligned run of 2 orbitals) all have 4. `pair_offsets`: each row is a permutation of 0 to 3; only its first pair_counts entries name pairs.
All inputs are finite; a program needn't handle non-finite values.
Results may differ from the reference program's by a relative error of at most 0.00013.
Values sent between devices are 32-bit elements; how exact they have to be, the bound alone decides.
A program may use at most 64 MiB of HBM per device.

```python
import math
import jax
import jax.numpy as jnp
from jax import lax

B = 32
ORB_DEV = 2
PMAX = 4
MEAN_PAIRS = 2
GROUP = 4
SMAX = 8
CYCLES = 2
SWEEPS = 4
ORBITALS = 16


def draw_orbitals(key, part):
    return jnp.clip(jax.random.normal(key, (ORBITALS, B, B * B), jnp.float32), -6.0, 6.0)


def draw_pair_counts(key, part):
    block_size = GROUP * ORB_DEV
    remaining = block_size - ORB_DEV
    surplus = MEAN_PAIRS * block_size - PMAX * ORB_DEV - remaining
    group_total = ORBITALS // block_size
    pick_count = max(surplus - 1, 1)

    def one_group(group_key):
        first_key, second_key = jax.random.split(group_key)
        busiest = jax.random.randint(first_key, (), 0, GROUP)
        chosen = jax.random.randint(second_key, (pick_count,), 0, remaining)
        usable = jnp.arange(pick_count)[:, None] < surplus - 1
        extras = jnp.sum(((chosen[:, None] == jnp.arange(remaining)[None, :]) & usable).astype(jnp.int32), axis=0)
        lowest = jnp.argmin(extras)
        extras = extras + (jnp.arange(remaining) == lowest).astype(jnp.int32)
        others = 1 + extras
        position = jnp.arange(block_size)
        holder = position // ORB_DEV
        place_index = jnp.clip(position - ORB_DEV * (holder > busiest).astype(jnp.int32), 0, remaining - 1)
        return jnp.where(holder == busiest, PMAX, others[place_index]).astype(jnp.int32)
    group_keys = jax.random.split(key, group_total)
    return jax.vmap(one_group)(group_keys).reshape(-1).astype(jnp.int32)


def set_ends(drawn, key, least, largest):
    longest = drawn.shape.index(max(drawn.shape))
    spots = []
    for shift in (0, 1):
        where = [jax.random.randint(jax.random.fold_in(key, axis), (), 0, length) for axis, length in enumerate(drawn.shape)]
        where[longest] = (where[longest] + shift) % drawn.shape[longest]
        spots.append(tuple(where))
    return drawn.at[spots[0]].set(least).at[spots[1]].set(largest)


def level_of(rng, dims, pieces, smallest, largest):
    loudness = 1.0
    for axis_at, parts in pieces:
        steps = jax.random.uniform(jax.random.fold_in(jax.random.fold_in(rng, 6), axis_at), (parts,), jnp.float32, smallest / len(pieces), largest / len(pieces))
        loudness = loudness * jnp.repeat(jnp.exp(steps), dims[axis_at] // parts).reshape((-1,) + (1,) * (len(dims) - 1 - axis_at))
    return loudness


def setup_inputs(seed: int = 0) -> dict:
    key_list = jax.random.split(jax.random.key(seed), 6)
    return {
        "orbitals": draw_orbitals(jax.random.fold_in(key_list[5], 71), 0),
        "dielectric": jnp.clip(jnp.exp(math.log(80.0) - 4.3820266 * jax.random.uniform(key_list[1], (ORBITALS, B, B * B), jnp.float32) ** level_of(key_list[1], (ORBITALS, B, B * B), ((0, 8), (1, 4)), -0.2, 0.2)), 1.0, 80.0),
        "pair_offsets": jax.vmap(lambda own: jax.random.permutation(own, PMAX))(jax.random.split(key_list[2], ORBITALS)).reshape((ORBITALS, PMAX)).astype(jnp.int32),
        "pair_counts": draw_pair_counts(jax.random.fold_in(key_list[5], 71), 0),
        "box_shift": set_ends(jax.random.randint(key_list[4], (ORBITALS,), 0, SMAX + 1), jax.random.fold_in(key_list[4], 1), 0, SMAX).astype(jnp.int32),
    }


FOURPI = 4.0 * 3.141592653589793
OMEGA = 0.8


def neighbour_cells(cube):
    padded = jnp.pad(cube, 1)
    return [padded[2:, 1:-1, 1:-1], padded[:-2, 1:-1, 1:-1], padded[1:-1, 2:, 1:-1],
            padded[1:-1, :-2, 1:-1], padded[1:-1, 1:-1, 2:], padded[1:-1, 1:-1, :-2]]


def diagonal_of(eps_cube, level_scale):
    summed = jnp.zeros_like(eps_cube)
    for eps_next in neighbour_cells(eps_cube):
        summed = summed + 0.5 * (eps_cube + eps_next)
    return level_scale * summed


def operate(values, eps_cube, diagonal, level_scale):
    weighted = jnp.zeros_like(values)
    for eps_next, val_next in zip(neighbour_cells(eps_cube), neighbour_cells(values)):
        weighted = weighted + 0.5 * (eps_cube + eps_next) * val_next
    return diagonal * values - level_scale * weighted


def coarsen(cube):
    edges = cube.shape
    return cube.reshape(edges[0] // 2, 2, edges[1] // 2, 2, edges[2] // 2, 2).mean(axis=(1, 3, 5))


def refine(cube):
    return jnp.repeat(jnp.repeat(jnp.repeat(cube, 2, axis=0), 2, axis=1), 2, axis=2)


def relaxed_step(values, rhs_level, level_data):
    eps_cube, diagonal, level_scale = level_data
    if values is None:
        return OMEGA * rhs_level / diagonal
    return values + OMEGA * (rhs_level - operate(values, eps_cube, diagonal, level_scale)) / diagonal


def multigrid_cycle(depth_index, values, rhs_level, levels):
    level_data = levels[depth_index]
    if depth_index == len(levels) - 1:
        for sweep_index in range(SWEEPS):
            values = relaxed_step(values, rhs_level, level_data)
        return values
    values = relaxed_step(values, rhs_level, level_data)
    residual = rhs_level - operate(values, level_data[0], level_data[1], level_data[2])
    correction = multigrid_cycle(depth_index + 1, None, coarsen(residual), levels)
    values = values + refine(correction)
    return relaxed_step(values, rhs_level, level_data)


def shift_rows(cube, row_offset):
    padded = jnp.pad(cube, ((0, 0), (SMAX, SMAX), (0, 0)))
    begin = (SMAX + row_offset).astype(jnp.int32)
    return lax.dynamic_slice(padded, (jnp.int32(0), begin, jnp.int32(0)), cube.shape)


def reference(orbitals, dielectric, pair_offsets, pair_counts, box_shift):
    orbital_count = pair_counts.shape[0]
    pair_total = MEAN_PAIRS * orbital_count
    starts = (jnp.cumsum(pair_counts) - pair_counts).astype(jnp.int32)
    serial = jnp.arange(pair_total, dtype=jnp.int32)
    first_orb = (jnp.sum((starts[None, :] <= serial[:, None]).astype(jnp.int32), axis=1) - 1).astype(jnp.int32)
    pair_rank = (serial - starts[first_orb]).astype(jnp.int32)
    second_orb = ((first_orb + 1 + pair_offsets[first_orb, pair_rank]) % orbital_count).astype(jnp.int32)
    orbital_cubes = orbitals.reshape(orbital_count, B, B, B)
    eps_cubes = dielectric.reshape(orbital_count, B, B, B)

    def one_pair(serial_index, summed):
        first_index = first_orb[serial_index]
        second_index = second_orb[serial_index]
        row_offset = (box_shift[first_index] - box_shift[second_index]).astype(jnp.int32)
        phi_first = orbital_cubes[first_index]
        moved = shift_rows(orbital_cubes[second_index], row_offset)
        rhs_fine = FOURPI * (phi_first * moved)
        eps_fine = eps_cubes[first_index]
        eps_half = coarsen(eps_fine)
        eps_quarter = coarsen(eps_half)
        levels = [(eps_fine, diagonal_of(eps_fine, 1.0), 1.0),
                  (eps_half, diagonal_of(eps_half, 0.25), 0.25),
                  (eps_quarter, diagonal_of(eps_quarter, 0.0625), 0.0625)]
        potential = None
        for cycle_index in range(CYCLES):
            potential = multigrid_cycle(0, potential, rhs_fine, levels)
        to_first = potential * moved
        to_second = shift_rows(potential * phi_first, -row_offset)
        summed = summed.at[first_index].add(-to_first)
        summed = summed.at[second_index].add(-to_second)
        return summed

    summed = lax.fori_loop(0, pair_total, one_pair, jnp.zeros(orbital_cubes.shape, jnp.float32))
    return summed.reshape(orbital_count, B, B * B)
```

```python
import functools

import jax
import jax.numpy as jnp
from jax import lax
from jax.experimental import pallas as pl
from jax.experimental.pallas import tpu as pltpu
from jax.sharding import PartitionSpec as P

PMAX = 4
SMAX = 8
CYCLES = 2
SWEEPS = 4
FOURPI = 4.0 * 3.141592653589793
OMEGA = 0.8
KEEP = 1.0 - OMEGA
LANES = 128
ROWS = 8
BEFORE = 2
AFTER = 2


def lane_roll(value, shift):
    return pltpu.roll(value, shift % LANES, value.ndim - 1)


def row_roll(value, shift):
    return pltpu.roll(value, shift % ROWS, value.ndim - 2)


def lane_bit(shape, bit):
    lane = lax.broadcasted_iota(jnp.int32, shape, len(shape) - 1)
    return ((lane >> bit) & 1) == 1


def z_up(value):
    return jnp.where(lane_bit(value.shape, 0), lane_roll(value, -31), lane_roll(value, -1))


def z_down(value):
    return jnp.where(lane_bit(value.shape, 0), lane_roll(value, 1), lane_roll(value, 31))


def swap_bits(tiles):
    tiles = list(tiles)
    for weight, bit in ((4, 6), (2, 5), (1, 0)):
        mask = lane_bit((ROWS, LANES), bit)
        step = 1 << bit
        for k in range(8):
            if not k & weight:
                a, b = tiles[k], tiles[k + weight]
                tiles[k] = jnp.where(mask, lane_roll(b, step), a)
                tiles[k + weight] = jnp.where(mask, b, lane_roll(a, -step))
    return tiles


def stack(parts):
    return jnp.concatenate([part[None] for part in parts], axis=0)


def kernel(
    n, G, own, N,
    orb_ref, eps_ref, off_ref, cnt_ref, shift_ref, out_ref,
    ibuf, ebuf, jbuf, moved, pbuf, tbuf, field, rhs, va, vb,
    kx, ky, kz, wt, dg, stage1, stage2, got1, got2,
    s_send, e_recv, i_recv, j_recv, f_send, f_recv, c_send, c_recv,
):
    per = G // own
    S = PMAX // per
    o = lax.axis_index("orb")
    g = lax.axis_index("grid")
    a_me = g // per
    h_me = lax.rem(g, per)

    def place(gr, p):
        reach = gr // per + (gr % per) * S + p + 1
        return reach // own, reach % own

    def at_orb(t):
        return lax.rem(o + (t + n), n)

    reach_t = [sorted({place(gr, p)[0] for p in range(S)} - {0}) for gr in range(G)]
    largest = max(max(ts) for ts in reach_t)

    barrier = pltpu.get_barrier_semaphore()

    def greet(orb, grid):
        pl.semaphore_signal(
            barrier, inc=1, device_id={"orb": orb, "grid": grid},
            device_id_type=pl.DeviceIdType.MESH,
        )

    for step in range(1, G):
        greet(o, lax.rem(g + step, G))
    greeted = G - 1
    for gr in range(G):
        for t in reach_t[gr]:
            greet(at_orb(-t), gr)
            greeted += 1
    expected = jnp.int32(greeted)
    for t in range(1, largest + 1):
        mine = functools.reduce(
            jnp.logical_or, [g == gr for gr in range(G) if t in reach_t[gr]]
        )

        @pl.when(mine)
        def _():
            for gr in range(G):
                greet(at_orb(t), gr)

        expected = expected + jnp.where(mine, G, 0).astype(jnp.int32)
    pl.semaphore_wait(barrier, expected)

    def send(src, dst, send_sem, recv_sem, orb, grid, is_self):
        def remote():
            return pltpu.make_async_remote_copy(
                src_ref=src, dst_ref=dst, send_sem=send_sem, recv_sem=recv_sem,
                device_id={"orb": orb, "grid": grid},
                device_id_type=pl.DeviceIdType.MESH,
            )

        if is_self is None:
            remote().start()
        else:
            @pl.when(is_self)
            def _():
                pltpu.make_async_copy(src, dst, recv_sem).start()

            @pl.when(jnp.logical_not(is_self))
            def _():
                remote().start()

        def finish():
            if is_self is None:
                remote().wait_send()
            else:
                @pl.when(jnp.logical_not(is_self))
                def _():
                    remote().wait_send()

        return finish

    pending = []
    count = 0
    mid = pl.ds(BEFORE * LANES, orb_ref.shape[2])
    for gr in range(G):
        pending.append(send(
            eps_ref.at[gr // per], ebuf.at[g], s_send.at[count], e_recv.at[g], o, gr, g == gr))
        count += 1
    for gr in range(G):
        for p in range(S):
            t, b = place(gr, p)
            pending.append(send(
                orb_ref.at[b], jbuf.at[p, g, :, mid], s_send.at[count], j_recv.at[p, g],
                at_orb(-t), gr, (g == gr) if t == 0 else None))
            count += 1
    for gr in range(G):
        pending.append(send(
            orb_ref.at[gr // per], ibuf.at[g], s_send.at[count], i_recv.at[g], o, gr, g == gr))
        count += 1

    first = o * own + a_me
    deltas, signs = [], []
    for p in range(S):
        distance = h_me * S + p + 1
        second = lax.rem(first + distance, N)
        deltas.append(shift_ref[first] - shift_ref[second])
        live = jnp.int32(0)
        for k in range(PMAX):
            hit = jnp.where(off_ref[first, k] == distance - 1, 1, 0)
            live = live + jnp.where(k < cnt_ref[first], hit, 0)
        signs.append(jnp.where(live > 0, -1.0, 0.0).astype(jnp.float32))

    wide = orb_ref.shape[2]
    tiles = wide // LANES
    for buf in (jbuf, pbuf):
        for p in range(S):
            for zh in range(G):
                buf[p, zh, :, 0 : BEFORE * LANES] = jnp.zeros((ROWS, BEFORE * LANES), jnp.float32)
                buf[p, zh, :, BEFORE * LANES + wide :] = jnp.zeros((ROWS, AFTER * LANES), jnp.float32)

    lane2 = lax.broadcasted_iota(jnp.int32, (ROWS, LANES), 1)

    def arrived(dst, sem):
        pltpu.make_async_copy(dst, dst, sem).wait()

    def load_shifted(buf, p, zh, delta):
        amount = jnp.full((ROWS, LANES), delta + SMAX, jnp.int32)
        bits = [((amount >> k) & 1) == 1 for k in range(5)]
        ext = [buf[p, zh, :, t * LANES : (t + 1) * LANES] for t in range(tiles + BEFORE + AFTER)]
        for k in (4, 3, 2):
            skip = 1 << (k - 2)
            ext = [
                jnp.where(bits[k], ext[t + skip], ext[t]) if t + skip < len(ext) else ext[t]
                for t in range(min(len(ext), tiles + skip))
            ]
        for k in (1, 0):
            step = 32 << k
            inner = lane2 < LANES - step
            turned = [lane_roll(value, -step) for value in ext]
            ext = [
                jnp.where(bits[k], jnp.where(inner, turned[t], turned[t + 1]) if t + 1 < len(ext) else turned[t], ext[t])
                for t in range(len(ext))
            ]
        return ext[:tiles]

    def to_blocked(src, dst_store):
        for zl in range(4):
            got = [
                src[k >> 1, pl.ds((k & 1) * 4 + zl, ROWS, stride=ROWS), :] for k in range(8)
            ]
            for k, value in enumerate(swap_bits(got)):
                dst_store(k >> 1, k & 1, zl, value)

    def put_tiles(dst, zh, slab):
        for yh in range(tiles):
            dst[zh, yh * ROWS : (yh + 1) * ROWS, :] = slab[:, yh * LANES : (yh + 1) * LANES]

    for zh in range(G):
        arrived(ebuf.at[zh], e_recv.at[zh])
        put_tiles(tbuf.at[S], zh, ebuf[zh])

    def store_eps(yl, x0, zl, value):
        field[yl, x0, zl] = value

    to_blocked(tbuf.at[S], store_eps)

    row2 = lax.broadcasted_iota(jnp.int32, (ROWS, LANES), 0)
    xh = (lane2 >> 1) & 15
    z8 = (lane2 >> 5) * 2 + (lane2 & 1)

    def keep(mask, value):
        return jnp.where(jnp.broadcast_to(mask, value.shape), value, 0.0)

    def face(scale, centre, beyond, mask=None):
        k = (0.5 * scale) * (centre + beyond)
        return k if mask is None else keep(mask, k)

    x_last, x_first = xh < 15, xh > 0
    y_last, y_first = row2 < 7, row2 > 0
    z_last, z_first = z8 < 7, z8 > 0

    for yl in range(4):
        e = field[yl]
        exp = stack([e[1], keep(x_last, lane_roll(e[0], -2))])
        exm = stack([keep(x_first, lane_roll(e[1], 2)), e[0]])
        eyp = field[yl + 1] if yl < 3 else keep(y_last, row_roll(field[0], -1))
        eym = field[yl - 1] if yl > 0 else keep(y_first, row_roll(field[3], 1))
        ezp = jnp.concatenate([e[:, 1:], keep(z_last, z_up(e[:, 0]))[:, None]], axis=1)
        ezm = jnp.concatenate([keep(z_first, z_down(e[:, 3]))[:, None], e[:, :3]], axis=1)
        diag = 3.0 * e + 0.5 * (((exp + exm) + (eyp + eym)) + (ezp + ezm))
        dg[yl] = diag
        wt[yl] = OMEGA / diag
        kxv = 0.5 * (e + exp)
        kx[yl, 0] = kxv[0]
        kx[yl, 1] = keep(x_last, kxv[1])
        kyv = 0.5 * (e + eyp)
        ky[yl] = kyv if yl < 3 else keep(y_last, kyv)
        kzv = 0.5 * (e + ezp)
        kz[yl, :, 0:3] = kzv[:, 0:3]
        kz[yl, :, 3] = keep(z_last, kzv[:, 3])

    def pair_sum(y0, y1):
        s = y0 + y1
        s = s[0] + s[1]
        return stack([s[0] + s[1], s[2] + s[3]])

    def to_quarter(mid_level):
        s = (mid_level[0, 0] + mid_level[0, 1]) + (mid_level[1, 0] + mid_level[1, 1])
        other = jnp.where(lane_bit(s.shape, 1), lane_roll(s, 2), lane_roll(s, -2))
        return 0.125 * (s + other)

    e1 = 0.125 * stack([pair_sum(field[0], field[1]), pair_sum(field[2], field[3])])

    def mid_y_up(v):
        return stack([v[1], row_roll(v[0], -1)])

    def mid_y_down(v):
        return stack([row_roll(v[1], 1), v[0]])

    def mid_z_up(v):
        return jnp.concatenate([v[:, 1:], z_up(v[:, 0])[:, None]], axis=1)

    def mid_z_down(v):
        return jnp.concatenate([z_down(v[:, 1])[:, None], v[:, :1]], axis=1)

    def mid_keep_y(mask, v, index):
        return stack([keep(mask, v[k]) if k == index else v[k] for k in range(2)])

    def mid_keep_z(mask, v, index):
        return jnp.concatenate(
            [(keep(mask, v[:, k]) if k == index else v[:, k])[:, None] for k in range(2)], axis=1)

    n1 = [
        keep(x_last, lane_roll(e1, -2)), keep(x_first, lane_roll(e1, 2)),
        mid_keep_y(y_last, mid_y_up(e1), 1), mid_keep_y(y_first, mid_y_down(e1), 0),
        mid_keep_z(z_last, mid_z_up(e1), 1), mid_keep_z(z_first, mid_z_down(e1), 0),
    ]
    w1 = OMEGA / (0.25 * (3.0 * e1 + 0.5 * (((n1[0] + n1[1]) + (n1[2] + n1[3])) + (n1[4] + n1[5]))))
    k1 = [face(0.25, e1, v) for v in n1]
    k1 = [
        keep(x_last, k1[0]), keep(x_first, k1[1]),
        mid_keep_y(y_last, k1[2], 1), mid_keep_y(y_first, k1[3], 0),
        mid_keep_z(z_last, k1[4], 1), mid_keep_z(z_first, k1[5], 0),
    ]
    e2 = to_quarter(e1)
    x2_last, x2_first = xh < 14, xh > 1
    masks2 = [x2_last, x2_first, y_last, y_first, z_last, z_first]

    def around2(v):
        return [lane_roll(v, -4), lane_roll(v, 4), row_roll(v, -1), row_roll(v, 1), z_up(v), z_down(v)]

    n2 = [keep(m, v) for m, v in zip(masks2, around2(e2))]
    w2 = OMEGA / (0.0625 * (3.0 * e2 + 0.5 * (((n2[0] + n2[1]) + (n2[2] + n2[3])) + (n2[4] + n2[5]))))
    k2 = [face(0.0625, e2, v, m) for m, v in zip(masks2, n2)]

    def weigh(ks, vs):
        t = [k * v for k, v in zip(ks, vs)]
        return ((t[0] + t[1]) + (t[2] + t[3])) + (t[4] + t[5])

    def off1(v):
        return weigh(k1, [lane_roll(v, -2), lane_roll(v, 2), mid_y_up(v), mid_y_down(v),
                          mid_z_up(v), mid_z_down(v)])

    def off2(v):
        return weigh(k2, around2(v))

    for zh in range(G):
        arrived(ibuf.at[zh], i_recv.at[zh])
        for p in range(S):
            arrived(jbuf.at[p, zh, :, mid], j_recv.at[p, zh])
            m = jnp.concatenate(load_shifted(jbuf, p, zh, deltas[p]), axis=1)
            moved[p, zh] = m
            put_tiles(tbuf.at[p], zh, FOURPI * (ibuf[zh] * m))
    for p in range(S):
        def store_rhs(yl, x0, zl, value):
            rhs[p, yl, x0, zl] = value

        to_blocked(tbuf.at[p], store_rhs)

    def off0(src, p, yl):
        v = src[p, yl]
        kxv, kzv = kx[yl], kz[yl]
        v0, v1 = v[0], v[1]
        xs = stack([kxv[0] * v1 + lane_roll(kxv[1] * v1, 2),
                    kxv[1] * lane_roll(v0, -2) + kxv[0] * v0])
        kv = kzv * v
        zs = kzv * jnp.concatenate([v[:, 1:], z_up(v[:, 0])[:, None]], axis=1)
        zs = zs + jnp.concatenate([z_down(kv[:, 3])[:, None], kv[:, :3]], axis=1)
        up = src[p, yl + 1] if yl < 3 else row_roll(src[p, 0], -1)
        ys = ky[yl] * up
        if yl > 0:
            ys = ys + ky[yl - 1] * src[p, yl - 1]
        else:
            ys = ys + row_roll(ky[3] * src[p, 3], 1)
        return xs + ys + zs

    def coarse(f1):
        u = w1 * f1
        f2 = to_quarter(KEEP * f1 + off1(u))
        t = w2 * f2
        for _ in range(SWEEPS - 1):
            t = KEEP * t + w2 * (f2 + off2(t))
        u = u + t
        return KEEP * u + w1 * (f1 + off1(u))

    def relax0(src, dst, p):
        for yl in range(4):
            dst[p, yl] = KEEP * src[p, yl] + wt[yl] * (rhs[p, yl] + off0(src, p, yl))

    for cycle in range(CYCLES):
        if cycle == 0:
            for p in range(S):
                for yl in range(4):
                    vb[p, yl] = wt[yl] * rhs[p, yl]
        else:
            for p in range(S):
                relax0(va, vb, p)
        coarse_rhs = []
        for p in range(S):
            rows = []
            for yh in range(2):
                res = []
                for yl in (2 * yh, 2 * yh + 1):
                    if cycle == 0:
                        res.append(KEEP * rhs[p, yl] + off0(vb, p, yl))
                    else:
                        res.append(rhs[p, yl] - dg[yl] * vb[p, yl] + off0(vb, p, yl))
                rows.append(pair_sum(res[0], res[1]))
            coarse_rhs.append(0.125 * stack(rows))
        corrections = [coarse(f1) for f1 in coarse_rhs]
        for p in range(S):
            for yl in range(4):
                c = corrections[p][yl // 2]
                grown = stack([c[0], c[0], c[1], c[1]])
                vb[p, yl] = vb[p, yl] + grown[None]
            relax0(vb, va, p)

    for p in range(S):
        for zl in range(4):
            got = [va[p, k >> 1, k & 1, zl] for k in range(8)]
            for k, value in enumerate(swap_bits(got)):
                tbuf[p, k >> 1, pl.ds((k & 1) * 4 + zl, ROWS, stride=ROWS), :] = value

    reaches = [a_me + h_me * S + p + 1 for p in range(S)]
    count = 0
    for zh in range(G):
        total = None
        for p in range(S):
            pot = jnp.concatenate(
                [tbuf[p, zh, yh * ROWS : (yh + 1) * ROWS, :] for yh in range(tiles)], axis=1)
            pot = signs[p] * pot
            term = pot * moved[p, zh]
            total = term if total is None else total + term
            pbuf[p, zh, :, mid] = pot * ibuf[zh]
            stage2[p, zh] = jnp.concatenate(load_shifted(pbuf, p, zh, -deltas[p]), axis=1)
            t = reaches[p] // own
            pending.append(send(
                stage2.at[p, zh], got2.at[g, p], c_send.at[p, zh], c_recv.at[g, p],
                lax.rem(o + t, n), zh, jnp.logical_and(t == 0, g == zh)))
        stage1[zh] = total
        pending.append(send(
            stage1.at[zh], got1.at[g], f_send.at[zh], f_recv.at[g], o, zh, g == zh))

    sums = [None] * own
    for gr in range(G):
        arrived(got1.at[gr], f_recv.at[gr])
        value = got1[gr]
        b = gr // per
        sums[b] = value if sums[b] is None else sums[b] + value
    for gr in range(G):
        for p in range(S):
            arrived(got2.at[gr, p], c_recv.at[gr, p])
            b = place(gr, p)[1]
            sums[b] = sums[b] + got2[gr, p]
    for b in range(own):
        out_ref[b] = sums[b]
    for finish in pending:
        finish()


def solution(mesh):
    n, G = mesh.shape["orb"], mesh.shape["grid"]

    def shards(orbitals, dielectric, pair_offsets, pair_counts, box_shift):
        own, rows, wide = orbitals.shape
        N = pair_counts.shape[0]
        S = own * PMAX // G
        padded = wide + (BEFORE + AFTER) * LANES
        f32 = jnp.float32
        blocked = (4, 2, 4, ROWS, LANES)
        smem = pl.BlockSpec(memory_space=pltpu.SMEM)
        hbm = pl.BlockSpec(memory_space=pl.ANY)
        dma = pltpu.SemaphoreType.DMA
        return pl.pallas_call(
            functools.partial(kernel, n, G, own, N),
            out_shape=jax.ShapeDtypeStruct(orbitals.shape, f32),
            in_specs=[hbm, hbm, smem, smem, smem],
            out_specs=pl.BlockSpec(memory_space=pltpu.VMEM),
            scratch_shapes=[
                pltpu.VMEM((G, rows, wide), f32),
                pltpu.VMEM((G, rows, wide), f32),
                pltpu.VMEM((S, G, rows, padded), f32),
                pltpu.VMEM((S, G, rows, wide), f32),
                pltpu.VMEM((S, G, rows, padded), f32),
                pltpu.VMEM((S + 1, G, rows * wide // LANES, LANES), f32),
                pltpu.VMEM(blocked, f32),
                pltpu.VMEM((S,) + blocked, f32),
                pltpu.VMEM((S,) + blocked, f32),
                pltpu.VMEM((S,) + blocked, f32),
                pltpu.VMEM(blocked, f32),
                pltpu.VMEM(blocked, f32),
                pltpu.VMEM(blocked, f32),
                pltpu.VMEM(blocked, f32),
                pltpu.VMEM(blocked, f32),
                pltpu.VMEM((G, rows, wide), f32),
                pltpu.VMEM((S, G, rows, wide), f32),
                pltpu.VMEM((G, rows, wide), f32),
                pltpu.VMEM((G, S, rows, wide), f32),
                dma((G * (S + 2),)),
                dma((G,)),
                dma((G,)),
                dma((S, G)),
                dma((G,)),
                dma((G,)),
                dma((S, G)),
                dma((G, S)),
            ],
            compiler_params=pltpu.CompilerParams(
                collective_id=0, has_side_effects=True, vmem_limit_bytes=24 * 1024 * 1024
            ),
        )(orbitals, dielectric, pair_offsets, pair_counts, box_shift)

    placed = (P("orb", "grid", None), P("orb", "grid", None), P(), P(), P())
    return jax.shard_map(
        shards, mesh=mesh, in_specs=placed, out_specs=P("orb", "grid", None), check_vma=False
    )
```

```python
import functools

import jax
import jax.numpy as jnp
from jax import lax
from jax.experimental import pallas as pl
from jax.experimental.pallas import tpu as pltpu
from jax.sharding import PartitionSpec as P

PMAX = 4
SMAX = 8
CYCLES = 2
SWEEPS = 4
FOURPI = 4.0 * 3.141592653589793
OMEGA = 0.8
KEEP = 1.0 - OMEGA
LANES = 128
ROWS = 8
BEFORE = 2
AFTER = 2


def lane_roll(value, shift):
    return pltpu.roll(value, shift % LANES, value.ndim - 1)


def row_roll(value, shift):
    return pltpu.roll(value, shift % ROWS, value.ndim - 2)


def lane_bit(shape, bit):
    lane = lax.broadcasted_iota(jnp.int32, shape, len(shape) - 1)
    return ((lane >> bit) & 1) == 1


def z_up(value):
    return jnp.where(lane_bit(value.shape, 0), lane_roll(value, -31), lane_roll(value, -1))


def z_down(value):
    return jnp.where(lane_bit(value.shape, 0), lane_roll(value, 1), lane_roll(value, 31))


def swap_bits(tiles):
    tiles = list(tiles)
    for weight, bit in ((4, 6), (2, 5), (1, 0)):
        mask = lane_bit((ROWS, LANES), bit)
        step = 1 << bit
        for k in range(8):
            if not k & weight:
                a, b = tiles[k], tiles[k + weight]
                tiles[k] = jnp.where(mask, lane_roll(b, step), a)
                tiles[k + weight] = jnp.where(mask, b, lane_roll(a, -step))
    return tiles


def stack(parts):
    return jnp.concatenate([part[None] for part in parts], axis=0)


def kernel(
    n, G, own, N,
    orb_ref, eps_ref, off_ref, cnt_ref, shift_ref, out_ref,
    ibuf, ebuf, jbuf, moved, pbuf, tbuf, field, rhs, va, vb,
    kx, ky, kz, wt, dg, stage1, stage2, got1, got2,
    s_send, e_recv, i_recv, j_recv, f_send, f_recv, c_send, c_recv,
):
    per = G // own
    S = PMAX // per
    o = lax.axis_index("orb")
    g = lax.axis_index("grid")
    a_me = g // per
    h_me = lax.rem(g, per)

    def place(gr, p):
        reach = gr // per + (gr % per) * S + p + 1
        return reach // own, reach % own

    def at_orb(t):
        return lax.rem(o + (t + n), n)

    reach_t = [sorted({place(gr, p)[0] for p in range(S)} - {0}) for gr in range(G)]
    largest = max(max(ts) for ts in reach_t)

    barrier = pltpu.get_barrier_semaphore()

    def greet(orb, grid):
        pl.semaphore_signal(
            barrier, inc=1, device_id={"orb": orb, "grid": grid},
            device_id_type=pl.DeviceIdType.MESH,
        )

    for step in range(1, G):
        greet(o, lax.rem(g + step, G))
    greeted = G - 1
    for gr in range(G):
        for t in reach_t[gr]:
            greet(at_orb(-t), gr)
            greeted += 1
    expected = jnp.int32(greeted)
    for t in range(1, largest + 1):
        mine = functools.reduce(
            jnp.logical_or, [g == gr for gr in range(G) if t in reach_t[gr]]
        )

        @pl.when(mine)
        def _():
            for gr in range(G):
                greet(at_orb(t), gr)

        expected = expected + jnp.where(mine, G, 0).astype(jnp.int32)
    pl.semaphore_wait(barrier, expected)

    def send(src, dst, send_sem, recv_sem, orb, grid, is_self):
        def remote():
            return pltpu.make_async_remote_copy(
                src_ref=src, dst_ref=dst, send_sem=send_sem, recv_sem=recv_sem,
                device_id={"orb": orb, "grid": grid},
                device_id_type=pl.DeviceIdType.MESH,
            )

        if is_self is None:
            remote().start()
        else:
            @pl.when(is_self)
            def _():
                pltpu.make_async_copy(src, dst, recv_sem).start()

            @pl.when(jnp.logical_not(is_self))
            def _():
                remote().start()

        def finish():
            if is_self is None:
                remote().wait_send()
            else:
                @pl.when(jnp.logical_not(is_self))
                def _():
                    remote().wait_send()

        return finish

    pending = []
    count = 0
    mid = pl.ds(BEFORE * LANES, orb_ref.shape[2])
    for gr in range(G):
        pending.append(send(
            eps_ref.at[gr // per], ebuf.at[g], s_send.at[count], e_recv.at[g], o, gr, g == gr))
        count += 1
    for gr in range(G):
        pending.append(send(
            orb_ref.at[gr // per], ibuf.at[g], s_send.at[count], i_recv.at[g], o, gr, g == gr))
        count += 1
    for p in range(S):
        for gr in range(G):
            t, b = place(gr, p)
            pending.append(send(
                orb_ref.at[b], jbuf.at[p, g, :, mid], s_send.at[count], j_recv.at[p, g],
                at_orb(-t), gr, (g == gr) if t == 0 else None))
            count += 1

    first = o * own + a_me
    deltas, signs = [], []
    for p in range(S):
        distance = h_me * S + p + 1
        second = lax.rem(first + distance, N)
        deltas.append(shift_ref[first] - shift_ref[second])
        live = jnp.int32(0)
        for k in range(PMAX):
            hit = jnp.where(off_ref[k, first] == distance - 1, 1, 0)
            live = live + jnp.where(k < cnt_ref[first], hit, 0)
        signs.append(jnp.where(live > 0, -1.0, 0.0).astype(jnp.float32))

    wide = orb_ref.shape[2]
    tiles = wide // LANES
    for buf in (jbuf, pbuf):
        for p in range(S):
            for zh in range(G):
                buf[p, zh, :, 0 : BEFORE * LANES] = jnp.zeros((ROWS, BEFORE * LANES), jnp.float32)
                buf[p, zh, :, BEFORE * LANES + wide :] = jnp.zeros((ROWS, AFTER * LANES), jnp.float32)

    lane2 = lax.broadcasted_iota(jnp.int32, (ROWS, LANES), 1)

    def arrived(dst, sem):
        pltpu.make_async_copy(dst, dst, sem).wait()

    def load_shifted(buf, p, zh, delta):
        amount = jnp.full((ROWS, LANES), delta + SMAX, jnp.int32)
        bits = [((amount >> k) & 1) == 1 for k in range(5)]
        ext = [buf[p, zh, :, t * LANES : (t + 1) * LANES] for t in range(tiles + BEFORE + AFTER)]
        for k in (4, 3, 2):
            skip = 1 << (k - 2)
            ext = [
                jnp.where(bits[k], ext[t + skip], ext[t]) if t + skip < len(ext) else ext[t]
                for t in range(min(len(ext), tiles + skip))
            ]
        for k in (1, 0):
            step = 32 << k
            inner = lane2 < LANES - step
            turned = [lane_roll(value, -step) for value in ext]
            ext = [
                jnp.where(bits[k], jnp.where(inner, turned[t], turned[t + 1]) if t + 1 < len(ext) else turned[t], ext[t])
                for t in range(len(ext))
            ]
        return ext[:tiles]

    def to_blocked(src, dst_store):
        for zl in range(4):
            got = [
                src[k >> 1, pl.ds((k & 1) * 4 + zl, ROWS, stride=ROWS), :] for k in range(8)
            ]
            for k, value in enumerate(swap_bits(got)):
                dst_store(k >> 1, k & 1, zl, value)

    def put_tiles(dst, zh, slab):
        for yh in range(tiles):
            dst[zh, yh * ROWS : (yh + 1) * ROWS, :] = slab[:, yh * LANES : (yh + 1) * LANES]

    for zh in range(G):
        arrived(ebuf.at[zh], e_recv.at[zh])
        put_tiles(tbuf.at[S], zh, ebuf[zh])

    def store_eps(yl, x0, zl, value):
        field[yl, x0, zl] = value

    to_blocked(tbuf.at[S], store_eps)

    row2 = lax.broadcasted_iota(jnp.int32, (ROWS, LANES), 0)
    xh = (lane2 >> 1) & 15
    z8 = (lane2 >> 5) * 2 + (lane2 & 1)

    def keep(mask, value):
        return jnp.where(jnp.broadcast_to(mask, value.shape), value, 0.0)

    def face(scale, centre, beyond, mask=None):
        k = (0.5 * scale) * (centre + beyond)
        return k if mask is None else keep(mask, k)

    x_last, x_first = xh < 15, xh > 0
    y_last, y_first = row2 < 7, row2 > 0
    z_last, z_first = z8 < 7, z8 > 0

    for yl in range(4):
        e = field[yl]
        exp = stack([e[1], keep(x_last, lane_roll(e[0], -2))])
        exm = stack([keep(x_first, lane_roll(e[1], 2)), e[0]])
        eyp = field[yl + 1] if yl < 3 else keep(y_last, row_roll(field[0], -1))
        eym = field[yl - 1] if yl > 0 else keep(y_first, row_roll(field[3], 1))
        ezp = jnp.concatenate([e[:, 1:], keep(z_last, z_up(e[:, 0]))[:, None]], axis=1)
        ezm = jnp.concatenate([keep(z_first, z_down(e[:, 3]))[:, None], e[:, :3]], axis=1)
        diag = 3.0 * e + 0.5 * (((exp + exm) + (eyp + eym)) + (ezp + ezm))
        dg[yl] = diag
        wt[yl] = OMEGA / diag
        kxv = 0.5 * (e + exp)
        kx[yl, 0] = kxv[0]
        kx[yl, 1] = keep(x_last, kxv[1])
        kyv = 0.5 * (e + eyp)
        ky[yl] = kyv if yl < 3 else keep(y_last, kyv)
        kzv = 0.5 * (e + ezp)
        kz[yl, :, 0:3] = kzv[:, 0:3]
        kz[yl, :, 3] = keep(z_last, kzv[:, 3])

    def pair_sum(y0, y1):
        s = y0 + y1
        s = s[0] + s[1]
        return stack([s[0] + s[1], s[2] + s[3]])

    def to_quarter(mid_level):
        s = (mid_level[0, 0] + mid_level[0, 1]) + (mid_level[1, 0] + mid_level[1, 1])
        other = jnp.where(lane_bit(s.shape, 1), lane_roll(s, 2), lane_roll(s, -2))
        return 0.125 * (s + other)

    e1 = 0.125 * stack([pair_sum(field[0], field[1]), pair_sum(field[2], field[3])])

    def mid_y_up(v):
        return stack([v[1], row_roll(v[0], -1)])

    def mid_y_down(v):
        return stack([row_roll(v[1], 1), v[0]])

    def mid_z_up(v):
        return jnp.concatenate([v[:, 1:], z_up(v[:, 0])[:, None]], axis=1)

    def mid_z_down(v):
        return jnp.concatenate([z_down(v[:, 1])[:, None], v[:, :1]], axis=1)

    def mid_keep_y(mask, v, index):
        return stack([keep(mask, v[k]) if k == index else v[k] for k in range(2)])

    def mid_keep_z(mask, v, index):
        return jnp.concatenate(
            [(keep(mask, v[:, k]) if k == index else v[:, k])[:, None] for k in range(2)], axis=1)

    n1 = [
        keep(x_last, lane_roll(e1, -2)), keep(x_first, lane_roll(e1, 2)),
        mid_keep_y(y_last, mid_y_up(e1), 1), mid_keep_y(y_first, mid_y_down(e1), 0),
        mid_keep_z(z_last, mid_z_up(e1), 1), mid_keep_z(z_first, mid_z_down(e1), 0),
    ]
    w1 = OMEGA / (0.25 * (3.0 * e1 + 0.5 * (((n1[0] + n1[1]) + (n1[2] + n1[3])) + (n1[4] + n1[5]))))
    k1 = [face(0.25, e1, v) for v in n1]
    k1 = [
        keep(x_last, k1[0]), keep(x_first, k1[1]),
        mid_keep_y(y_last, k1[2], 1), mid_keep_y(y_first, k1[3], 0),
        mid_keep_z(z_last, k1[4], 1), mid_keep_z(z_first, k1[5], 0),
    ]
    e2 = to_quarter(e1)
    x2_last, x2_first = xh < 14, xh > 1
    masks2 = [x2_last, x2_first, y_last, y_first, z_last, z_first]

    def around2(v):
        return [lane_roll(v, -4), lane_roll(v, 4), row_roll(v, -1), row_roll(v, 1), z_up(v), z_down(v)]

    n2 = [keep(m, v) for m, v in zip(masks2, around2(e2))]
    w2 = OMEGA / (0.0625 * (3.0 * e2 + 0.5 * (((n2[0] + n2[1]) + (n2[2] + n2[3])) + (n2[4] + n2[5]))))
    k2 = [face(0.0625, e2, v, m) for m, v in zip(masks2, n2)]

    def weigh(ks, vs):
        t = [k * v for k, v in zip(ks, vs)]
        return ((t[0] + t[1]) + (t[2] + t[3])) + (t[4] + t[5])

    def off1(v):
        return weigh(k1, [lane_roll(v, -2), lane_roll(v, 2), mid_y_up(v), mid_y_down(v),
                          mid_z_up(v), mid_z_down(v)])

    def off2(v):
        return weigh(k2, around2(v))

    def off0(src, p, yl):
        v = src[p, yl]
        kxv, kzv = kx[yl], kz[yl]
        v0, v1 = v[0], v[1]
        xs = stack([kxv[0] * v1 + lane_roll(kxv[1] * v1, 2),
                    kxv[1] * lane_roll(v0, -2) + kxv[0] * v0])
        kv = kzv * v
        zs = kzv * jnp.concatenate([v[:, 1:], z_up(v[:, 0])[:, None]], axis=1)
        zs = zs + jnp.concatenate([z_down(kv[:, 3])[:, None], kv[:, :3]], axis=1)
        up = src[p, yl + 1] if yl < 3 else row_roll(src[p, 0], -1)
        ys = ky[yl] * up
        if yl > 0:
            ys = ys + ky[yl - 1] * src[p, yl - 1]
        else:
            ys = ys + row_roll(ky[3] * src[p, 3], 1)
        return xs + ys + zs

    def coarse(f1):
        u = w1 * f1
        f2 = to_quarter(KEEP * f1 + off1(u))
        t = w2 * f2
        for _ in range(SWEEPS - 1):
            t = KEEP * t + w2 * (f2 + off2(t))
        u = u + t
        return KEEP * u + w1 * (f1 + off1(u))

    def relax0(src, dst, p):
        for yl in range(4):
            dst[p, yl] = KEEP * src[p, yl] + wt[yl] * (rhs[p, yl] + off0(src, p, yl))

    def solve(p):
        for cycle in range(CYCLES):
            if cycle == 0:
                for yl in range(4):
                    vb[p, yl] = wt[yl] * rhs[p, yl]
            else:
                relax0(va, vb, p)
            rows = []
            for yh in range(2):
                res = []
                for yl in (2 * yh, 2 * yh + 1):
                    if cycle == 0:
                        res.append(KEEP * rhs[p, yl] + off0(vb, p, yl))
                    else:
                        res.append(rhs[p, yl] - dg[yl] * vb[p, yl] + off0(vb, p, yl))
                rows.append(pair_sum(res[0], res[1]))
            correction = coarse(0.125 * stack(rows))
            for yl in range(4):
                c = correction[yl // 2]
                grown = stack([c[0], c[0], c[1], c[1]])
                vb[p, yl] = vb[p, yl] + grown[None]
            relax0(vb, va, p)

    for p in range(S):
        for zh in range(G):
            if p == 0:
                arrived(ibuf.at[zh], i_recv.at[zh])
            arrived(jbuf.at[p, zh, :, mid], j_recv.at[p, zh])
            m = jnp.concatenate(load_shifted(jbuf, p, zh, deltas[p]), axis=1)
            moved[p, zh] = m
            put_tiles(tbuf.at[p], zh, FOURPI * (ibuf[zh] * m))

        def store_rhs(yl, x0, zl, value):
            rhs[p, yl, x0, zl] = value

        to_blocked(tbuf.at[p], store_rhs)
        solve(p)
        for zl in range(4):
            got = [va[p, k >> 1, k & 1, zl] for k in range(8)]
            for k, value in enumerate(swap_bits(got)):
                tbuf[p, k >> 1, pl.ds((k & 1) * 4 + zl, ROWS, stride=ROWS), :] = value
        t = (a_me + h_me * S + p + 1) // own
        for zh in range(G):
            pot = jnp.concatenate(
                [tbuf[p, zh, yh * ROWS : (yh + 1) * ROWS, :] for yh in range(tiles)], axis=1)
            pot = signs[p] * pot
            pbuf[p, zh, :, mid] = pot * ibuf[zh]
            stage2[p, zh] = jnp.concatenate(load_shifted(pbuf, p, zh, -deltas[p]), axis=1)
            pending.append(send(
                stage2.at[p, zh], got2.at[g, p], c_send.at[p, zh], c_recv.at[g, p],
                lax.rem(o + t, n), zh, jnp.logical_and(t == 0, g == zh)))
            term = pot * moved[p, zh]
            stage1[zh] = term if p == 0 else stage1[zh] + term
            if p == S - 1:
                pending.append(send(
                    stage1.at[zh], got1.at[g], f_send.at[zh], f_recv.at[g], o, zh, g == zh))

    sums = [None] * own
    for gr in range(G):
        arrived(got1.at[gr], f_recv.at[gr])
        value = got1[gr]
        b = gr // per
        sums[b] = value if sums[b] is None else sums[b] + value
    for gr in range(G):
        for p in range(S):
            arrived(got2.at[gr, p], c_recv.at[gr, p])
            b = place(gr, p)[1]
            sums[b] = sums[b] + got2[gr, p]
    for b in range(own):
        out_ref[b] = sums[b]
    for finish in pending:
        finish()


def solution(mesh):
    n, G = mesh.shape["orb"], mesh.shape["grid"]

    def shards(orbitals, dielectric, pair_offsets, pair_counts, box_shift):
        own, rows, wide = orbitals.shape
        N = pair_counts.shape[0]
        S = own * PMAX // G
        padded = wide + (BEFORE + AFTER) * LANES
        f32 = jnp.float32
        blocked = (4, 2, 4, ROWS, LANES)
        smem = pl.BlockSpec(memory_space=pltpu.SMEM)
        hbm = pl.BlockSpec(memory_space=pltpu.HBM)
        dma = pltpu.SemaphoreType.DMA
        return pl.pallas_call(
            functools.partial(kernel, n, G, own, N),
            out_shape=jax.ShapeDtypeStruct(orbitals.shape, f32),
            in_specs=[hbm, hbm, smem, smem, smem],
            out_specs=pl.BlockSpec(memory_space=pltpu.VMEM),
            scratch_shapes=[
                pltpu.VMEM((G, rows, wide), f32),
                pltpu.VMEM((G, rows, wide), f32),
                pltpu.VMEM((S, G, rows, padded), f32),
                pltpu.VMEM((S, G, rows, wide), f32),
                pltpu.VMEM((S, G, rows, padded), f32),
                pltpu.VMEM((S + 1, G, rows * wide // LANES, LANES), f32),
                pltpu.VMEM(blocked, f32),
                pltpu.VMEM((S,) + blocked, f32),
                pltpu.VMEM((S,) + blocked, f32),
                pltpu.VMEM((S,) + blocked, f32),
                pltpu.VMEM(blocked, f32),
                pltpu.VMEM(blocked, f32),
                pltpu.VMEM(blocked, f32),
                pltpu.VMEM(blocked, f32),
                pltpu.VMEM(blocked, f32),
                pltpu.VMEM((G, rows, wide), f32),
                pltpu.VMEM((S, G, rows, wide), f32),
                pltpu.VMEM((G, rows, wide), f32),
                pltpu.VMEM((G, S, rows, wide), f32),
                dma((G * (S + 2),)),
                dma((G,)),
                dma((G,)),
                dma((S, G)),
                dma((G,)),
                dma((G,)),
                dma((S, G)),
                dma((G, S)),
            ],
            compiler_params=pltpu.CompilerParams(
                collective_id=0, has_side_effects=True, vmem_limit_bytes=63 * 1024 * 1024
            ),
        )(orbitals, dielectric, pair_offsets.T, pair_counts, box_shift)

    placed = (P("orb", "grid", None), P("orb", "grid", None), P(), P(), P())
    return jax.shard_map(
        shards, mesh=mesh, in_specs=placed, out_specs=P("orb", "grid", None), check_vma=False
    )
```

```python
import functools

import jax
import jax.numpy as jnp
from jax import lax
from jax.experimental import pallas as pl
from jax.experimental.pallas import tpu as pltpu
from jax.sharding import PartitionSpec as P

PMAX = 4
SMAX = 8
CYCLES = 2
SWEEPS = 4
FOURPI = 4.0 * 3.141592653589793
OMEGA = 0.8
KEEP = 1.0 - OMEGA
LANES = 128
ROWS = 8
BEFORE = 2
AFTER = 2


def lane_roll(value, shift):
    return pltpu.roll(value, shift % LANES, value.ndim - 1)


def row_roll(value, shift):
    return pltpu.roll(value, shift % ROWS, value.ndim - 2)


def lane_bit(shape, bit):
    lane = lax.broadcasted_iota(jnp.int32, shape, len(shape) - 1)
    return ((lane >> bit) & 1) == 1


def z_up(value):
    return jnp.where(lane_bit(value.shape, 0), lane_roll(value, -31), lane_roll(value, -1))


def z_down(value):
    return jnp.where(lane_bit(value.shape, 0), lane_roll(value, 1), lane_roll(value, 31))


def swap_bits(tiles):
    tiles = list(tiles)
    for weight, bit in ((4, 6), (2, 5), (1, 0)):
        mask = lane_bit((ROWS, LANES), bit)
        step = 1 << bit
        for k in range(8):
            if not k & weight:
                a, b = tiles[k], tiles[k + weight]
                tiles[k] = jnp.where(mask, lane_roll(b, step), a)
                tiles[k + weight] = jnp.where(mask, b, lane_roll(a, -step))
    return tiles


def stack(parts):
    return jnp.concatenate([part[None] for part in parts], axis=0)


def kernel(
    n, G, own, N,
    orb_ref, eps_ref, off_ref, cnt_ref, shift_ref, out_ref,
    ibuf, ebuf, jbuf, moved, pbuf, tbuf, field, rhs, va, vb,
    kx, ky, kz, wt, dg, stage1, stage2, got1, got2,
    b_send, b_recv, j_send, j_recv, f_send, f_recv, c_send, c_recv,
):
    per = G // own
    S = PMAX // per
    o = lax.axis_index("orb")
    g = lax.axis_index("grid")
    a_me = g // per
    h_me = lax.rem(g, per)

    def place(gr, p):
        reach = gr // per + (gr % per) * S + p + 1
        return reach // own, reach % own

    def at_orb(t):
        return lax.rem(o + (t + n), n)

    reach_t = [sorted({place(gr, p)[0] for p in range(S)} - {0}) for gr in range(G)]
    largest = max(max(ts) for ts in reach_t)

    barrier = pltpu.get_barrier_semaphore()

    def greet(orb, grid):
        pl.semaphore_signal(
            barrier, inc=1, device_id={"orb": orb, "grid": grid},
            device_id_type=pl.DeviceIdType.MESH,
        )

    for step in range(1, G):
        greet(o, lax.rem(g + step, G))
    greeted = G - 1
    for gr in range(G):
        for t in reach_t[gr]:
            greet(at_orb(-t), gr)
            greeted += 1
    expected = jnp.int32(greeted)
    for t in range(1, largest + 1):
        mine = functools.reduce(
            jnp.logical_or, [g == gr for gr in range(G) if t in reach_t[gr]]
        )

        @pl.when(mine)
        def _():
            for gr in range(G):
                greet(at_orb(t), gr)

        expected = expected + jnp.where(mine, G, 0).astype(jnp.int32)
    pl.semaphore_wait(barrier, expected)

    def remote(src, dst, send_sem, recv_sem, orb, grid):
        pltpu.make_async_remote_copy(
            src_ref=src, dst_ref=dst, send_sem=send_sem, recv_sem=recv_sem,
            device_id={"orb": orb, "grid": grid}, device_id_type=pl.DeviceIdType.MESH,
        ).start()

    def local(src, dst, recv_sem):
        pltpu.make_async_copy(src, dst, recv_sem).start()

    def arrived(whole, sem):
        pltpu.make_async_copy(whole, whole, sem).wait()

    def own_slot(p):
        found = [gr for gr in range(G) if place(gr, p)[0] == 0]
        return found[0] if found else None

    mid = pl.ds(BEFORE * LANES, orb_ref.shape[2])
    others = [lax.rem(g + step, G) for step in range(1, G)]
    for field_ref, buf, which in ((eps_ref, ebuf, 0), (orb_ref, ibuf, 1)):
        for gr in others:
            remote(field_ref.at[gr // per], buf.at[g], b_send.at[which], b_recv.at[which], o, gr)
        local(field_ref.at[a_me], buf.at[g], b_recv.at[which])
    for p in range(S):
        for gr in range(G):
            t, b = place(gr, p)
            src, dst = orb_ref.at[b], jbuf.at[p, g, :, mid]

            def to_other(src=src, dst=dst, t=t, gr=gr, p=p):
                remote(src, dst, j_send.at[p], j_recv.at[p], at_orb(-t), gr)

            if gr == own_slot(p):
                pl.when(g != gr)(to_other)

                @pl.when(g == gr)
                def _(src=src, dst=dst, p=p):
                    local(src, dst, j_recv.at[p])
            else:
                to_other()

    first = o * own + a_me
    deltas, signs = [], []
    for p in range(S):
        distance = h_me * S + p + 1
        second = lax.rem(first + distance, N)
        deltas.append(shift_ref[first] - shift_ref[second])
        live = jnp.int32(0)
        for k in range(PMAX):
            hit = jnp.where(off_ref[k, first] == distance - 1, 1, 0)
            live = live + jnp.where(k < cnt_ref[first], hit, 0)
        signs.append(jnp.where(live > 0, -1.0, 0.0).astype(jnp.float32))

    wide = orb_ref.shape[2]
    tiles = wide // LANES
    for buf in (jbuf, pbuf):
        for p in range(S):
            for zh in range(G):
                buf[p, zh, :, 0 : BEFORE * LANES] = jnp.zeros((ROWS, BEFORE * LANES), jnp.float32)
                buf[p, zh, :, BEFORE * LANES + wide :] = jnp.zeros((ROWS, AFTER * LANES), jnp.float32)

    lane2 = lax.broadcasted_iota(jnp.int32, (ROWS, LANES), 1)

    def load_shifted(buf, p, zh, delta):
        amount = jnp.full((ROWS, LANES), delta + SMAX, jnp.int32)
        bits = [((amount >> k) & 1) == 1 for k in range(5)]
        ext = [buf[p, zh, :, t * LANES : (t + 1) * LANES] for t in range(tiles + BEFORE + AFTER)]
        for k in (4, 3, 2):
            skip = 1 << (k - 2)
            ext = [
                jnp.where(bits[k], ext[t + skip], ext[t]) if t + skip < len(ext) else ext[t]
                for t in range(min(len(ext), tiles + skip))
            ]
        for k in (1, 0):
            step = 32 << k
            inner = lane2 < LANES - step
            turned = [lane_roll(value, -step) for value in ext]
            ext = [
                jnp.where(bits[k], jnp.where(inner, turned[t], turned[t + 1]) if t + 1 < len(ext) else turned[t], ext[t])
                for t in range(len(ext))
            ]
        return ext[:tiles]

    def to_blocked(src, dst_store):
        for zl in range(4):
            got = [
                src[k >> 1, pl.ds((k & 1) * 4 + zl, ROWS, stride=ROWS), :] for k in range(8)
            ]
            for k, value in enumerate(swap_bits(got)):
                dst_store(k >> 1, k & 1, zl, value)

    def put_tiles(dst, zh, slab):
        for yh in range(tiles):
            dst[zh, yh * ROWS : (yh + 1) * ROWS, :] = slab[:, yh * LANES : (yh + 1) * LANES]

    arrived(ebuf, b_recv.at[0])
    for zh in range(G):
        put_tiles(tbuf.at[S], zh, ebuf[zh])

    def store_eps(yl, x0, zl, value):
        field[yl, x0, zl] = value

    to_blocked(tbuf.at[S], store_eps)

    row2 = lax.broadcasted_iota(jnp.int32, (ROWS, LANES), 0)
    xh = (lane2 >> 1) & 15
    z8 = (lane2 >> 5) * 2 + (lane2 & 1)

    def keep(mask, value):
        return jnp.where(jnp.broadcast_to(mask, value.shape), value, 0.0)

    def face(scale, centre, beyond, mask=None):
        k = (0.5 * scale) * (centre + beyond)
        return k if mask is None else keep(mask, k)

    x_last, x_first = xh < 15, xh > 0
    y_last, y_first = row2 < 7, row2 > 0
    z_last, z_first = z8 < 7, z8 > 0

    for yl in range(4):
        e = field[yl]
        exp = stack([e[1], keep(x_last, lane_roll(e[0], -2))])
        exm = stack([keep(x_first, lane_roll(e[1], 2)), e[0]])
        eyp = field[yl + 1] if yl < 3 else keep(y_last, row_roll(field[0], -1))
        eym = field[yl - 1] if yl > 0 else keep(y_first, row_roll(field[3], 1))
        ezp = jnp.concatenate([e[:, 1:], keep(z_last, z_up(e[:, 0]))[:, None]], axis=1)
        ezm = jnp.concatenate([keep(z_first, z_down(e[:, 3]))[:, None], e[:, :3]], axis=1)
        diag = 3.0 * e + 0.5 * (((exp + exm) + (eyp + eym)) + (ezp + ezm))
        dg[yl] = diag
        wt[yl] = OMEGA / diag
        kxv = 0.5 * (e + exp)
        kx[yl, 0] = kxv[0]
        kx[yl, 1] = keep(x_last, kxv[1])
        kyv = 0.5 * (e + eyp)
        ky[yl] = kyv if yl < 3 else keep(y_last, kyv)
        kzv = 0.5 * (e + ezp)
        kz[yl, :, 0:3] = kzv[:, 0:3]
        kz[yl, :, 3] = keep(z_last, kzv[:, 3])

    def pair_sum(y0, y1):
        s = y0 + y1
        s = s[0] + s[1]
        return stack([s[0] + s[1], s[2] + s[3]])

    def to_quarter(mid_level):
        s = (mid_level[0, 0] + mid_level[0, 1]) + (mid_level[1, 0] + mid_level[1, 1])
        other = jnp.where(lane_bit(s.shape, 1), lane_roll(s, 2), lane_roll(s, -2))
        return 0.125 * (s + other)

    e1 = 0.125 * stack([pair_sum(field[0], field[1]), pair_sum(field[2], field[3])])

    def mid_y_up(v):
        return stack([v[1], row_roll(v[0], -1)])

    def mid_y_down(v):
        return stack([row_roll(v[1], 1), v[0]])

    def mid_z_up(v):
        return jnp.concatenate([v[:, 1:], z_up(v[:, 0])[:, None]], axis=1)

    def mid_z_down(v):
        return jnp.concatenate([z_down(v[:, 1])[:, None], v[:, :1]], axis=1)

    def mid_keep_y(mask, v, index):
        return stack([keep(mask, v[k]) if k == index else v[k] for k in range(2)])

    def mid_keep_z(mask, v, index):
        return jnp.concatenate(
            [(keep(mask, v[:, k]) if k == index else v[:, k])[:, None] for k in range(2)], axis=1)

    n1 = [
        keep(x_last, lane_roll(e1, -2)), keep(x_first, lane_roll(e1, 2)),
        mid_keep_y(y_last, mid_y_up(e1), 1), mid_keep_y(y_first, mid_y_down(e1), 0),
        mid_keep_z(z_last, mid_z_up(e1), 1), mid_keep_z(z_first, mid_z_down(e1), 0),
    ]
    w1 = OMEGA / (0.25 * (3.0 * e1 + 0.5 * (((n1[0] + n1[1]) + (n1[2] + n1[3])) + (n1[4] + n1[5]))))
    k1 = [face(0.25, e1, v) for v in n1]
    k1 = [
        keep(x_last, k1[0]), keep(x_first, k1[1]),
        mid_keep_y(y_last, k1[2], 1), mid_keep_y(y_first, k1[3], 0),
        mid_keep_z(z_last, k1[4], 1), mid_keep_z(z_first, k1[5], 0),
    ]
    e2 = to_quarter(e1)
    x2_last, x2_first = xh < 14, xh > 1
    masks2 = [x2_last, x2_first, y_last, y_first, z_last, z_first]

    def around2(v):
        return [lane_roll(v, -4), lane_roll(v, 4), row_roll(v, -1), row_roll(v, 1), z_up(v), z_down(v)]

    n2 = [keep(m, v) for m, v in zip(masks2, around2(e2))]
    w2 = OMEGA / (0.0625 * (3.0 * e2 + 0.5 * (((n2[0] + n2[1]) + (n2[2] + n2[3])) + (n2[4] + n2[5]))))
    k2 = [face(0.0625, e2, v, m) for m, v in zip(masks2, n2)]

    def weigh(ks, vs):
        t = [k * v for k, v in zip(ks, vs)]
        return ((t[0] + t[1]) + (t[2] + t[3])) + (t[4] + t[5])

    def off1(v):
        return weigh(k1, [lane_roll(v, -2), lane_roll(v, 2), mid_y_up(v), mid_y_down(v),
                          mid_z_up(v), mid_z_down(v)])

    def off2(v):
        return weigh(k2, around2(v))

    def off0(src, p, yl):
        v = src[p, yl]
        kxv, kzv = kx[yl], kz[yl]
        v0, v1 = v[0], v[1]
        xs = stack([kxv[0] * v1 + lane_roll(kxv[1] * v1, 2),
                    kxv[1] * lane_roll(v0, -2) + kxv[0] * v0])
        kv = kzv * v
        zs = kzv * jnp.concatenate([v[:, 1:], z_up(v[:, 0])[:, None]], axis=1)
        zs = zs + jnp.concatenate([z_down(kv[:, 3])[:, None], kv[:, :3]], axis=1)
        up = src[p, yl + 1] if yl < 3 else row_roll(src[p, 0], -1)
        ys = ky[yl] * up
        if yl > 0:
            ys = ys + ky[yl - 1] * src[p, yl - 1]
        else:
            ys = ys + row_roll(ky[3] * src[p, 3], 1)
        return xs + ys + zs

    def coarse(f1):
        u = w1 * f1
        f2 = to_quarter(KEEP * f1 + off1(u))
        t = w2 * f2
        for _ in range(SWEEPS - 1):
            t = KEEP * t + w2 * (f2 + off2(t))
        u = u + t
        return KEEP * u + w1 * (f1 + off1(u))

    def relax0(src, dst, p):
        for yl in range(4):
            dst[p, yl] = KEEP * src[p, yl] + wt[yl] * (rhs[p, yl] + off0(src, p, yl))

    def solve(p):
        for cycle in range(CYCLES):
            if cycle == 0:
                for yl in range(4):
                    vb[p, yl] = wt[yl] * rhs[p, yl]
            else:
                relax0(va, vb, p)
            rows = []
            for yh in range(2):
                res = []
                for yl in (2 * yh, 2 * yh + 1):
                    if cycle == 0:
                        res.append(KEEP * rhs[p, yl] + off0(vb, p, yl))
                    else:
                        res.append(rhs[p, yl] - dg[yl] * vb[p, yl] + off0(vb, p, yl))
                rows.append(pair_sum(res[0], res[1]))
            correction = coarse(0.125 * stack(rows))
            for yl in range(4):
                c = correction[yl // 2]
                grown = stack([c[0], c[0], c[1], c[1]])
                vb[p, yl] = vb[p, yl] + grown[None]
            relax0(vb, va, p)

    for p in range(S):
        if p == 0:
            arrived(ibuf, b_recv.at[1])
        arrived(jbuf.at[p, :, :, mid], j_recv.at[p])
        for zh in range(G):
            m = jnp.concatenate(load_shifted(jbuf, p, zh, deltas[p]), axis=1)
            moved[p, zh] = m
            put_tiles(tbuf.at[p], zh, FOURPI * (ibuf[zh] * m))

        def store_rhs(yl, x0, zl, value):
            rhs[p, yl, x0, zl] = value

        to_blocked(tbuf.at[p], store_rhs)
        solve(p)
        for zl in range(4):
            got = [va[p, k >> 1, k & 1, zl] for k in range(8)]
            for k, value in enumerate(swap_bits(got)):
                tbuf[p, k >> 1, pl.ds((k & 1) * 4 + zl, ROWS, stride=ROWS), :] = value
        t = (a_me + h_me * S + p + 1) // own
        for zh in range(G):
            pot = jnp.concatenate(
                [tbuf[p, zh, yh * ROWS : (yh + 1) * ROWS, :] for yh in range(tiles)], axis=1)
            pot = signs[p] * pot
            pbuf[p, zh, :, mid] = pot * ibuf[zh]
            stage2[p, zh] = jnp.concatenate(load_shifted(pbuf, p, zh, -deltas[p]), axis=1)
            def to_other(p=p, zh=zh, t=t):
                remote(stage2.at[p, zh], got2.at[g, p], c_send.at[p], c_recv, lax.rem(o + t, n), zh)

            if zh == own_slot(p):
                pl.when(g != zh)(to_other)

                @pl.when(g == zh)
                def _(p=p, zh=zh):
                    local(stage2.at[p, zh], got2.at[g, p], c_recv)
            else:
                to_other()
            term = pot * moved[p, zh]
            stage1[zh] = term if p == 0 else stage1[zh] + term
    for zh in others:
        remote(stage1.at[zh], got1.at[g], f_send, f_recv, o, zh)
    local(stage1.at[g], got1.at[g], f_recv)

    arrived(ebuf.at[pl.ds(0, G - 1)], b_send.at[0])
    arrived(ibuf.at[pl.ds(0, G - 1)], b_send.at[1])
    for whole, sem in ((ebuf, j_send), (stage1, c_send)):
        for p in range(S):
            gr = own_slot(p)
            if gr is None:
                arrived(whole, sem.at[p])
            else:
                @pl.when(g != gr)
                def _(whole=whole, sem=sem, p=p):
                    arrived(whole, sem.at[p])

                @pl.when(g == gr)
                def _(whole=whole, sem=sem, p=p):
                    arrived(whole.at[pl.ds(0, G - 1)], sem.at[p])
    arrived(stage1.at[pl.ds(0, G - 1)], f_send)

    sums = [None] * own
    arrived(got2, c_recv)
    for gr in range(G):
        for p in range(S):
            b = place(gr, p)[1]
            value = got2[gr, p]
            sums[b] = value if sums[b] is None else sums[b] + value
    arrived(got1, f_recv)
    for gr in range(G):
        b = gr // per
        sums[b] = sums[b] + got1[gr]
    for b in range(own):
        out_ref[b] = sums[b]


def solution(mesh):
    n, G = mesh.shape["orb"], mesh.shape["grid"]

    def shards(orbitals, dielectric, pair_offsets, pair_counts, box_shift):
        own, rows, wide = orbitals.shape
        N = pair_counts.shape[0]
        S = own * PMAX // G
        padded = wide + (BEFORE + AFTER) * LANES
        f32 = jnp.float32
        blocked = (4, 2, 4, ROWS, LANES)
        smem = pl.BlockSpec(memory_space=pltpu.SMEM)
        hbm = pl.BlockSpec(memory_space=pltpu.HBM)
        dma = pltpu.SemaphoreType.DMA
        return pl.pallas_call(
            functools.partial(kernel, n, G, own, N),
            out_shape=jax.ShapeDtypeStruct(orbitals.shape, f32),
            in_specs=[hbm, hbm, smem, smem, smem],
            out_specs=pl.BlockSpec(memory_space=pltpu.VMEM),
            scratch_shapes=[
                pltpu.VMEM((G, rows, wide), f32),
                pltpu.VMEM((G, rows, wide), f32),
                pltpu.VMEM((S, G, rows, padded), f32),
                pltpu.VMEM((S, G, rows, wide), f32),
                pltpu.VMEM((S, G, rows, padded), f32),
                pltpu.VMEM((S + 1, G, rows * wide // LANES, LANES), f32),
                pltpu.VMEM(blocked, f32),
                pltpu.VMEM((S,) + blocked, f32),
                pltpu.VMEM((S,) + blocked, f32),
                pltpu.VMEM((S,) + blocked, f32),
                pltpu.VMEM(blocked, f32),
                pltpu.VMEM(blocked, f32),
                pltpu.VMEM(blocked, f32),
                pltpu.VMEM(blocked, f32),
                pltpu.VMEM(blocked, f32),
                pltpu.VMEM((G, rows, wide), f32),
                pltpu.VMEM((S, G, rows, wide), f32),
                pltpu.VMEM((G, rows, wide), f32),
                pltpu.VMEM((G, S, rows, wide), f32),
                dma((2,)),
                dma((2,)),
                dma((S,)),
                dma((S,)),
                dma(()),
                dma(()),
                dma((S,)),
                dma(()),
            ],
            compiler_params=pltpu.CompilerParams(
                collective_id=0, has_side_effects=True, vmem_limit_bytes=63 * 1024 * 1024
            ),
        )(orbitals, dielectric, pair_offsets.T, pair_counts, box_shift)

    placed = (P("orb", "grid", None), P("orb", "grid", None), P(), P(), P())
    return jax.shard_map(
        shards, mesh=mesh, in_specs=placed, out_specs=P("orb", "grid", None), check_vma=False
    )
```
